32 devices in a mesh: row: 4 (over z), col: 4 (over y, x), dp: 2 (over core).
Axes of the slice: x: 2, y: 2, z: 4, core: 2. Of those that a mesh axis runs over, the one named last changes fastest.
Arguments:
- tokens: bfloat16 [2048, 8192], P(('col', 'dp'), 'row'), may hold values from -6 to 6
- out_grad: bfloat16 [2048, 8192], P(('col', 'dp'), 'row'), may hold values from -6 to 6
- weight_in: bfloat16 [8192, 16384], P('row', 'col'), may hold values from -0.0625 to 0.0625
- weight_out: bfloat16 [16384, 8192], P('col', 'row'), may hold values from -0.046875 to 0.046875
Outputs:
- mixed: bfloat16 [2048, 8192], P(('col', 'dp'), 'row')
- token_grad: bfloat16 [2048, 8192], P(('col', 'dp'), 'row')
- grad_in: float32 [8192, 16384], P('row', ('col', 'dp'))
- grad_out: float32 [16384, 8192], P(('col', 'dp'), 'row')
The draws below stay inside these ranges and needn't reach their ends.
All inputs are finite; a program needn't handle non-finite values.
Results may differ from the reference program's by a relative error of at most 0.035.
Values may be sent and summed in bfloat16 or wider, within the bound.
A program may use at most 256 MiB of HBM per device.

```python
import math
import jax
import jax.numpy as jnp
from jax import lax

D = 8192
FF = 16384
TOKENS = 2048
D_PART = 2048
FF_PART = 4096


def steps_of(key, shape, split, least, high):
    def one(position, blocks):
        draws = jax.random.uniform(jax.random.fold_in(jax.random.fold_in(key, 6), position), (blocks,), jnp.float32, least / len(split), high / len(split))
        return jnp.repeat(jnp.exp(draws), shape[position] // blocks).reshape((-1,) + (1,) * (len(shape) - position - 1))

    loudness = one(*split[0])
    for cut in split[1:]:
        loudness = loudness * one(*cut)
    return loudness


def bell_draw(rng, shape, spread, reach, shards=(), dtype=jnp.bfloat16):
    values = spread * jax.random.normal(rng, shape, jnp.float32)
    if shards:
        values = values * steps_of(rng, shape, shards, -0.22, 0.18)
    return jnp.clip(values, -reach, reach).astype(dtype)


def setup_inputs(seed: int = 0) -> dict:
    splits = jax.random.split(jax.random.key(seed), 5)
    tokens = bell_draw(splits[0], (TOKENS, D), 1.0, 6.0, ((0, 8), (1, 4)))
    out_grad = bell_draw(splits[1], (TOKENS, D), 1.0, 6.0, ((0, 8), (1, 4)))
    weight_in = bell_draw(splits[2], (D, FF), D ** -0.5, 0.0625, ((0, 4), (1, 4)))
    weight_out = bell_draw(splits[3], (FF, D), FF ** -0.5, 0.046875, ((0, 4), (1, 4)))
    return {"tokens": tokens, "out_grad": out_grad, "weight_in": weight_in, "weight_out": weight_out}


def gelu_parts(pre):
    cdf = 0.5 * (1.0 + jax.scipy.special.erf(pre * (1.0 / math.sqrt(2.0))))
    activated = pre * cdf
    slope = cdf + pre * jnp.exp(-0.5 * pre * pre) * (1.0 / math.sqrt(2.0 * math.pi))
    return (activated, slope)

def summed_blocks(left, right, width):
    parts = left.shape[1] // width
    total = jnp.zeros((left.shape[0], right.shape[1]), jnp.float32)
    for index in range(parts):
        term = jnp.dot(left[:, index * width:(index + 1) * width], right[index * width:(index + 1) * width], preferred_element_type=jnp.float32)
        rounded = lax.optimization_barrier(term.astype(jnp.bfloat16))
        total = total + rounded.astype(jnp.float32)
    return total

def reference(tokens, out_grad, weight_in, weight_out):
    pre = summed_blocks(tokens, weight_in, D_PART)
    activated, slope = gelu_parts(pre)
    act = activated.astype(jnp.bfloat16)
    mixed = summed_blocks(act, weight_out, FF_PART).astype(jnp.bfloat16)
    back = summed_blocks(out_grad, weight_out.T, D_PART)
    dpre = (back * slope).astype(jnp.bfloat16)
    token_grad = summed_blocks(dpre, weight_in.T, FF_PART).astype(jnp.bfloat16)
    factor = 1.0 / math.sqrt(TOKENS)
    grad_in = jnp.dot(tokens.T, dpre, preferred_element_type=jnp.float32) * factor
    grad_out = jnp.dot(act.T, out_grad, preferred_element_type=jnp.float32) * factor
    return (mixed, token_grad, grad_in, grad_out)
```

```python
import math

import jax
import jax.numpy as jnp
from jax import lax
from jax.sharding import PartitionSpec as P

F32, BF16 = jnp.float32, jnp.bfloat16


def gelu_parts(pre):
    cdf = 0.5 * (1.0 + jax.scipy.special.erf(pre * (1.0 / math.sqrt(2.0))))
    activated = pre * cdf
    slope = cdf + pre * jnp.exp(-0.5 * pre * pre) * (1.0 / math.sqrt(2.0 * math.pi))
    return (activated, slope)


class LineSum:
    def __init__(self, axis):
        self.axis = axis
        self.size = lax.axis_size(axis)
        self.me = lax.axis_index(axis)
        self.moving = None
        self.gathered = None
        self.pending = None

    def shift(self, pair):
        n = self.size
        right = [(i, i + 1) for i in range(n - 1)]
        left = [(i + 1, i) for i in range(n - 1)]
        return (lax.ppermute(pair[0], self.axis, right), lax.ppermute(pair[1], self.axis, left))

    def tick(self, s, parts):
        n, z = self.size, self.me
        sends = []
        for direction in range(2):
            at = z if direction == 0 else n - 1 - z
            send = None if self.moving is None else self.moving[direction]
            if parts is not None:
                shard = jnp.clip(n - s + at, 0, n - 1)
                shard = shard if direction == 0 else n - 1 - shard
                own = lax.dynamic_index_in_dim(parts, shard, 0, keepdims=False)
                own = jnp.where(at < s, own, jnp.zeros_like(own))
                send = own if send is None else (send.astype(F32) + own.astype(F32)).astype(BF16)
            sends.append(send)
        self.moving = self.shift(sends)
        if self.pending is not None and s <= n - 2:
            self.gathered.append(self.moving)

    def collect(self):
        n, z = self.size, self.me
        own, got = self.pending, self.gathered
        full = jnp.zeros((n,) + own.shape, own.dtype)
        full = lax.dynamic_update_index_in_dim(full, own, z, 0)
        for a in range(1, n):
            piece = jnp.where(z >= a, got[a - 1][0], got[n - a - 1][1])
            full = lax.dynamic_update_index_in_dim(full, piece, lax.rem(z - a + n, n), 0)
        return full.reshape((-1,) + own.shape[1:])

    def steps(self, parts, finish):
        n = self.size
        for s in range(1, n):
            self.tick(s, parts)
            if s == max(n - 2, 1) and self.pending is not None:
                yield self.collect()
            else:
                yield None
        if parts is None:
            return
        own = lax.dynamic_index_in_dim(parts, self.me, 0, keepdims=False).astype(F32)
        total = own + self.moving[0].astype(F32) + self.moving[1].astype(F32)
        self.pending = finish(total)
        self.moving = self.shift((self.pending, self.pending))
        self.gathered = [self.moving]
        yield None

    def drain(self):
        n = self.size
        for s in range(1, n - 1):
            self.moving = self.shift(self.moving)
            self.gathered.append(self.moving)
            yield None
        yield self.collect()


def shards(tokens, out_grad, weight_in, weight_out):
    cols = lax.axis_size("col")
    rows = lax.axis_size("row")
    factor = 1.0 / math.sqrt(tokens.shape[0] * cols * lax.axis_size("dp"))
    hidden = weight_in.shape[1]
    half = hidden // 2
    core = lax.axis_index("dp")

    def swap(x, k):
        return x if k == 0 else lax.ppermute(x, "col", [(i, i ^ k) for i in range(cols)])

    def other(x):
        return lax.ppermute(x, "dp", [(0, 1), (1, 0)])

    def both(x):
        mine = lax.dynamic_slice_in_dim(x, core * half, half, 1)
        theirs = lax.dynamic_slice_in_dim(x, (1 - core) * half, half, 1)
        return [mine, other(theirs)]

    def cut(x):
        return x.astype(BF16).reshape(rows, -1, hidden)

    tok = [swap(tokens, k) for k in range(cols)]
    cot = [swap(out_grad, k) for k in range(cols)]
    tok_all = [(t, other(t)) for t in tok]
    cot_all = [(t, other(t)) for t in cot]

    slopes, act, dpre = {}, {}, {}
    mixed_parts, token_parts = {}, {}

    def forward(k):
        parts = cut(jnp.dot(tok[k], weight_in, preferred_element_type=F32))

        def finish(total):
            activated, slopes[k] = gelu_parts(total)
            return activated.astype(BF16)

        return parts, finish

    def backward(k):
        parts = cut(
            lax.dot_general(cot[k], weight_out, (((1,), (1,)), ((), ())), preferred_element_type=F32)
        )
        return parts, lambda total: (total * slopes[k]).astype(BF16)

    def done(kind, k, block):
        if kind == 0:
            act[k] = both(block)
            part = jnp.dot(block, weight_out, preferred_element_type=F32)
            mixed_parts[k] = swap(part.astype(BF16), k)
        else:
            dpre[k] = both(block)
            part = lax.dot_general(
                block, weight_in, (((1,), (1,)), ((), ())), preferred_element_type=F32
            )
            token_parts[k] = swap(part.astype(BF16), k)

    def chain(first):
        line = LineSum("row")
        last = None
        for kind in range(2):
            for k in range(first, cols, 2):
                parts, finish = (forward, backward)[kind](k)
                for block in line.steps(parts, finish):
                    if block is not None:
                        done(*last, block)
                    yield
                last = (kind, k)
        for block in line.drain():
            if block is not None:
                done(*last, block)
            yield

    running = [chain(first) for first in range(min(2, cols))]
    while running:
        still = []
        for one in running:
            try:
                next(one)
                still.append(one)
            except StopIteration:
                pass
        running = still

    def summed(parts):
        total = parts[0].astype(F32)
        for k in range(1, cols):
            total = total + parts[k].astype(F32)
        return total.astype(BF16)

    def joined(pairs, ks):
        return jnp.concatenate([x for k in ks for x in pairs[k]], axis=0)

    def across(left, right):
        return lax.dot_general(left, right, (((0,), (0,)), ((), ())), preferred_element_type=F32)

    every = range(cols)
    grad_out = across(joined(act, every), joined(cot_all, every)) * factor
    early, late = range(cols // 2), range(cols // 2, cols)
    grad_in = across(joined(tok_all, early), joined(dpre, early))
    grad_in = (grad_in + across(joined(tok_all, late), joined(dpre, late))) * factor
    return (summed(mixed_parts), summed(token_parts), grad_in, grad_out)


def solution(mesh):
    placed = (P(("col", "dp"), "row"), P(("col", "dp"), "row"), P("row", "col"), P("col", "row"))
    return jax.shard_map(
        shards,
        mesh=mesh,
        in_specs=placed,
        out_specs=(
            P(("col", "dp"), "row"),
            P(("col", "dp"), "row"),
            P("row", ("col", "dp")),
            P(("col", "dp"), "row"),
        ),
        check_vma=False,
    )
```

```python
import functools
import math

import jax
import jax.numpy as jnp
from jax import lax
from jax.experimental import pallas as pl
from jax.experimental.pallas import tpu as pltpu
from jax.sharding import PartitionSpec as P

F32, BF16 = jnp.float32, jnp.bfloat16
MESH = pl.DeviceIdType.MESH


def gelu_parts(pre):
    cdf = 0.5 * (1.0 + jax.scipy.special.erf(pre * (1.0 / math.sqrt(2.0))))
    activated = pre * cdf
    slope = cdf + pre * jnp.exp(-0.5 * pre * pre) * (1.0 / math.sqrt(2.0 * math.pi))
    return (activated, slope)


def line_kernel(
    n, cols, tok_ref, cot_ref, win_ref, wout_ref, ptok_ref, pcot_ref, full_ref,
    parts, outgo, land, stage, slope, tok_buf, win_buf, wout_buf,
    send_sem, recv_sem, gsend_sem, grecv_sem, local_sem, load_sem,
):
    rows, hidden = tok_ref.shape[0], win_ref.shape[1]
    shard, width = rows // n, hidden // n
    z, me = lax.axis_index("row"), lax.axis_index("col")
    strip = min(512, hidden)

    barrier = pltpu.get_barrier_semaphore()

    @pl.when(z > 0)
    def _():
        pl.semaphore_signal(barrier, inc=1, device_id={"row": z - 1}, device_id_type=MESH)

    @pl.when(z < n - 1)
    def _():
        pl.semaphore_signal(barrier, inc=1, device_id={"row": z + 1}, device_id_type=MESH)

    for k in range(1, cols):
        peer = lax.rem(me + k, cols)
        pl.semaphore_signal(barrier, inc=1, device_id={"col": peer}, device_id_type=MESH)

    @pl.when(jnp.logical_or(z == 0, z == n - 1))
    def _():
        pl.semaphore_wait(barrier, cols)

    @pl.when(jnp.logical_and(z > 0, z < n - 1))
    def _():
        pl.semaphore_wait(barrier, cols + 1)

    sources, panels = (tok_ref, cot_ref), (ptok_ref, pcot_ref)

    def gather(kind, k):
        return pltpu.make_async_remote_copy(
            src_ref=sources[kind], dst_ref=panels[kind].at[k],
            send_sem=gsend_sem.at[kind, k], recv_sem=grecv_sem.at[kind, k],
            device_id={"col": lax.rem(me + cols - k, cols)}, device_id_type=MESH,
        )

    for kind in range(2):
        for k in range(1, cols):
            gather(kind, k).start()
    own_copies = [
        pltpu.make_async_copy(sources[kind], panels[kind].at[0], local_sem.at[kind])
        for kind in range(2)
    ]
    for copy in own_copies:
        copy.start()
    for copy in own_copies:
        copy.wait()

    def weights_copy(kind, part):
        if kind == 0:
            src = win_ref.at[:, pl.ds(part * width, width)]
            return pltpu.make_async_copy(src, win_buf, load_sem.at[0])
        src = wout_ref.at[pl.ds(part * width, width), :]
        return pltpu.make_async_copy(src, wout_buf, load_sem.at[0])

    def tokens_copy(kind, k):
        return pltpu.make_async_copy(panels[kind].at[k], tok_buf, load_sem.at[1])

    def load(kind, k, part):
        weights_copy(kind, part).start()
        if part == 0:
            for slot in range(1, cols):
                @pl.when(k == slot)
                def _():
                    gather(kind, slot).wait_recv()
            tokens_copy(kind, k).start()

    def multiply(kind, k, part, half, chain):
        weights_copy(kind, part).wait()
        if part == 0:
            tokens_copy(kind, k).wait()
        step = min(width, 256)

        @pl.loop(0, width // step)
        def _(i):
            at = pl.multiple_of(i * step, step)
            if kind == 0:
                out = jnp.dot(tok_buf[...], win_buf[:, pl.ds(at, step)], preferred_element_type=F32)
            else:
                out = lax.dot_general(
                    tok_buf[...], wout_buf[pl.ds(at, step), :], (((1,), (1,)), ((), ())),
                    preferred_element_type=F32,
                )
            to = pl.multiple_of(part * width + i * step, step)
            parts[half, chain, :, :, pl.ds(to, step)] = out.astype(BF16).reshape(n, shard, step)

    def place(d):
        return z if d == 0 else n - 1 - z

    def real(d, q):
        return q if d == 0 else n - 1 - q

    def forms(s, d):
        p = place(d)
        if s == n:
            return p < n - 1, p >= 1
        return jnp.logical_and(p < n - 1, p < s), jnp.logical_and(p >= 1, p - 1 < s)

    def passes_on(s, d):
        p = place(d)
        return jnp.logical_and(p < n - 1, p >= s), jnp.logical_and(p >= 1, p - 1 >= s)

    def both(a, b):
        return jnp.logical_and(a, b)

    def copy_of(src, dst, s, c, d):
        return pltpu.make_async_remote_copy(
            src_ref=src, dst_ref=dst, send_sem=send_sem.at[s - 1, c, d],
            recv_sem=recv_sem.at[s - 1, c, d],
            device_id={"row": z + 1 if d == 0 else z - 1}, device_id_type=MESH,
        )

    def any_copy(s, c, d):
        return copy_of(stage.at[c], stage.at[c], s, c, d)

    def active(g, s, d, sending):
        which = 0 if sending else 1
        fresh = both(forms(s, d)[which], both(g >= 0, g < cols))
        if s > n - 2:
            return fresh
        old = both(passes_on(s, d)[which], both(g >= 1, g <= cols))
        return jnp.logical_or(fresh, old)

    def wait_recv(g, s, c):
        for d in range(2):
            @pl.when(active(g, s, d, False))
            def _():
                any_copy(s, c, d).wait_recv()

    def wait_send(g, s, c):
        for d in range(2):
            @pl.when(active(g, s, d, True))
            def _():
                any_copy(s, c, d).wait_send()

    def arrive(g, s, c):
        if s == 1:
            wait_recv(g - 1, n, c)
        else:
            wait_recv(g, s - 1, c)

    def pass_on(g, s, c):
        for d in range(2):
            @pl.when(both(passes_on(s, d)[0], g >= 1))
            def _():
                slot = full_ref.at[2 * (g - 1) + c, real(d, place(d) - s)]
                copy_of(slot, slot, s, c, d).start()

    def tick(g, s, c):
        half = lax.rem(g, 2)
        arrive(g, s, c)
        wait_send(g - 1, s, c)
        if s <= n - 2:
            pass_on(g, s, c)
        for d in range(2):
            @pl.when(forms(s, d)[0])
            def _():
                p = place(d)
                j = real(d, n - s + p)

                if s > 1:
                    @pl.when(p >= 1)
                    def _():
                        @pl.loop(0, hidden // strip)
                        def _(i):
                            at = pl.ds(pl.multiple_of(i * strip, strip), strip)
                            own = parts[half, c, j, :, at].astype(F32)
                            got = land[s - 2, c, d, :, at].astype(F32)
                            outgo[s - 1, c, d, :, at] = (own + got).astype(BF16)

                @pl.when(p == 0)
                def _():
                    outgo[s - 1, c, d] = parts[half, c, j]

                copy_of(outgo.at[s - 1, c, d], land.at[s - 1, c, d], s, c, d).start()

    def finish(g, c):
        half = lax.rem(g, 2)
        arrive(g, n, c)
        wait_send(g - 1, n, c)
        k = lax.rem(2 * g + c, cols)

        def total(at):
            own = parts[half, c, z, :, at].astype(F32)
            from_left = jnp.where(z > 0, land[n - 2, c, 0, :, at].astype(F32), 0.0)
            from_right = jnp.where(z < n - 1, land[n - 2, c, 1, :, at].astype(F32), 0.0)
            return own + from_left + from_right

        @pl.when(2 * g < cols)
        def _():
            @pl.loop(0, hidden // strip)
            def _(i):
                at = pl.ds(pl.multiple_of(i * strip, strip), strip)
                activated, steep = gelu_parts(total(at))
                slope[k, :, at] = steep
                stage[c, :, at] = activated.astype(BF16)

        @pl.when(2 * g >= cols)
        def _():
            @pl.loop(0, hidden // strip)
            def _(i):
                at = pl.ds(pl.multiple_of(i * strip, strip), strip)
                stage[c, :, at] = (total(at) * slope[k, :, at]).astype(BF16)

        slot = full_ref.at[2 * g + c, z]
        for d in range(2):
            @pl.when(forms(n, d)[0])
            def _():
                copy_of(stage.at[c], slot, n, c, d).start()
        keep = pltpu.make_async_copy(stage.at[c], slot, local_sem.at[0])
        keep.start()
        keep.wait()

    for c in range(2):
        for part in range(n):
            load(0, c, part)
            multiply(0, c, part, 0, c)
        if c == 0:
            tick(jnp.int32(0), 1, 0)

    @pl.loop(0, cols)
    def _(g):
        for s in range(1, n + 1):
            for c in range(2):
                piece = (s - 1) * 2 + c
                chain, part = piece // n, piece % n
                k = lax.rem(2 * (g + 1) + chain, cols)
                ahead_in = 2 * (g + 1) < cols
                ahead_out = both(2 * (g + 1) >= cols, g < cols - 1)
                for kind, ahead in enumerate((ahead_in, ahead_out)):
                    @pl.when(ahead)
                    def _():
                        load(kind, k, part)
                if s == n:
                    finish(g, c)
                elif s == 1 and c == 0:
                    @pl.when(g > 0)
                    def _():
                        tick(g, s, c)
                else:
                    tick(g, s, c)
                for kind, ahead in enumerate((ahead_in, ahead_out)):
                    @pl.when(ahead)
                    def _():
                        multiply(kind, k, part, lax.rem(g + 1, 2), chain)

    last = jnp.int32(cols)
    for s in range(1, n - 1):
        for c in range(2):
            arrive(last, s, c)
            wait_send(last - 1, s, c)
            pass_on(last, s, c)
    for c in range(2):
        if n > 2:
            wait_recv(last, n - 2, c)
        else:
            wait_recv(last - 1, n, c)
        for s in range(1, n - 1):
            wait_send(last, s, c)
        for s in (n - 1, n):
            wait_send(last - 1, s, c)
    for kind in range(2):
        for k in range(1, cols):
            gather(kind, k).wait_send()


def line_call(n, cols, tokens, out_grad, weight_in, weight_out):
    rows, depth = tokens.shape
    hidden = weight_in.shape[1]
    shard, width = rows // n, hidden // n
    return pl.pallas_call(
        functools.partial(line_kernel, n, cols),
        out_shape=[
            jax.ShapeDtypeStruct((cols, rows, depth), BF16),
            jax.ShapeDtypeStruct((cols, rows, depth), BF16),
            jax.ShapeDtypeStruct((2 * cols, n, shard, hidden), BF16),
        ],
        in_specs=[pl.BlockSpec(memory_space=pl.ANY)] * 4,
        out_specs=[pl.BlockSpec(memory_space=pl.ANY)] * 3,
        scratch_shapes=[
            pltpu.VMEM((2, 2, n, shard, hidden), BF16),
            pltpu.VMEM((n - 1, 2, 2, shard, hidden), BF16),
            pltpu.VMEM((n - 1, 2, 2, shard, hidden), BF16),
            pltpu.VMEM((2, shard, hidden), BF16),
            pltpu.VMEM((cols, shard, hidden), F32),
            pltpu.VMEM((rows, depth), BF16),
            pltpu.VMEM((depth, width), BF16),
            pltpu.VMEM((width, depth), BF16),
            pltpu.SemaphoreType.DMA((n, 2, 2)),
            pltpu.SemaphoreType.DMA((n, 2, 2)),
            pltpu.SemaphoreType.DMA((2, cols)),
            pltpu.SemaphoreType.DMA((2, cols)),
            pltpu.SemaphoreType.DMA((2,)),
            pltpu.SemaphoreType.DMA((2,)),
        ],
        compiler_params=pltpu.CompilerParams(
            collective_id=0, has_side_effects=True, vmem_limit_bytes=56 * 2**20
        ),
    )(tokens, out_grad, weight_in, weight_out)


def shards(tokens, out_grad, weight_in, weight_out):
    cols, n = lax.axis_size("col"), lax.axis_size("row")
    factor = 1.0 / math.sqrt(tokens.shape[0] * cols * lax.axis_size("dp"))
    hidden = weight_in.shape[1]
    half = hidden // 2
    core = lax.axis_index("dp")
    tok, cot, full = line_call(n, cols, tokens, out_grad, weight_in, weight_out)
    full = full.reshape(2, -1, hidden)
    tok, cot = tok.reshape(-1, tok.shape[-1]), cot.reshape(-1, cot.shape[-1])
    act, dpre = full[0], full[1]

    def home(part):
        part = part.astype(BF16).reshape(cols, -1, part.shape[-1])
        total = part[0].astype(F32)
        for k in range(1, cols):
            ring = [(i, (i + k) % cols) for i in range(cols)]
            total = total + lax.ppermute(part[k], "col", ring).astype(F32)
        return total.astype(BF16)

    def other(x):
        return lax.ppermute(x, "dp", [(0, 1), (1, 0)])

    def units(x):
        mine = lax.dynamic_slice_in_dim(x, core * half, half, 1)
        theirs = lax.dynamic_slice_in_dim(x, (1 - core) * half, half, 1)
        return jnp.concatenate([mine, other(theirs)], axis=0)

    def across(left, right):
        return lax.dot_general(left, right, (((0,), (0,)), ((), ())), preferred_element_type=F32)

    mixed = home(jnp.dot(act, weight_out, preferred_element_type=F32))
    token_grad = home(
        lax.dot_general(dpre, weight_in, (((1,), (1,)), ((), ())), preferred_element_type=F32)
    )
    grad_out = across(units(act), jnp.concatenate([cot, other(cot)], axis=0)) * factor
    grad_in = across(jnp.concatenate([tok, other(tok)], axis=0), units(dpre)) * factor
    return (mixed, token_grad, grad_in, grad_out)


def solution(mesh):
    placed = (P(("col", "dp"), "row"), P(("col", "dp"), "row"), P("row", "col"), P("col", "row"))
    return jax.shard_map(
        shards,
        mesh=mesh,
        in_specs=placed,
        out_specs=(
            P(("col", "dp"), "row"),
            P(("col", "dp"), "row"),
            P("row", ("col", "dp")),
            P(("col", "dp"), "row"),
        ),
        check_vma=False,
    )
```

```python
import functools
import math

import jax
import jax.numpy as jnp
from jax import lax
from jax.experimental import pallas as pl
from jax.experimental.pallas import tpu as pltpu
from jax.sharding import PartitionSpec as P

F32, BF16 = jnp.float32, jnp.bfloat16
MESH = pl.DeviceIdType.MESH


def gelu_parts(pre):
    cdf = 0.5 * (1.0 + jax.scipy.special.erf(pre * (1.0 / math.sqrt(2.0))))
    activated = pre * cdf
    slope = cdf + pre * jnp.exp(-0.5 * pre * pre) * (1.0 / math.sqrt(2.0 * math.pi))
    return (activated, slope)


def line_kernel(
    n, cols, tok_ref, cot_ref, win_ref, wout_ref, ptok_ref, pcot_ref,
    act_ref, dpre_ref, uact_ref, udpre_ref, parts, outgo, land, stage, slope, tok_buf, win_buf, wout_buf,
    send_sem, recv_sem, gsend_sem, grecv_sem, local_sem, load_sem,
    psend_sem, precv_sem, usend_sem, urecv_sem, ulocal_sem,
):
    rows, hidden = tok_ref.shape[0], win_ref.shape[1]
    shard, width = rows // n, hidden // n
    z, me = lax.axis_index("row"), lax.axis_index("col")
    strip = min(512, hidden)
    core, units = lax.axis_index("dp"), hidden // 2

    barrier = pltpu.get_barrier_semaphore()

    @pl.when(z > 0)
    def _():
        pl.semaphore_signal(barrier, inc=1, device_id={"row": z - 1}, device_id_type=MESH)

    @pl.when(z < n - 1)
    def _():
        pl.semaphore_signal(barrier, inc=1, device_id={"row": z + 1}, device_id_type=MESH)

    pl.semaphore_signal(barrier, inc=1, device_id={"dp": 1 - core}, device_id_type=MESH)
    for k in range(1, cols):
        peer = lax.rem(me + k, cols)
        pl.semaphore_signal(barrier, inc=1, device_id={"col": peer}, device_id_type=MESH)

    @pl.when(jnp.logical_or(z == 0, z == n - 1))
    def _():
        pl.semaphore_wait(barrier, cols + 1)

    @pl.when(jnp.logical_and(z > 0, z < n - 1))
    def _():
        pl.semaphore_wait(barrier, cols + 2)

    sources, panels = (tok_ref, cot_ref), (ptok_ref, pcot_ref)

    fulls, halves = (act_ref, dpre_ref), (uact_ref, udpre_ref)

    def partner(kind, k):
        return pltpu.make_async_remote_copy(
            src_ref=panels[kind].at[0, k], dst_ref=panels[kind].at[1, k],
            send_sem=psend_sem.at[kind, k], recv_sem=precv_sem.at[kind, k],
            device_id={"dp": 1 - core}, device_id_type=MESH,
        )

    def unit_send(kind, k):
        theirs = pl.ds(pl.multiple_of((1 - core) * units, units), units)
        return pltpu.make_async_remote_copy(
            src_ref=fulls[kind].at[k, :, :, theirs], dst_ref=halves[kind].at[1, k],
            send_sem=usend_sem.at[kind, k], recv_sem=urecv_sem.at[kind, k],
            device_id={"dp": 1 - core}, device_id_type=MESH,
        )

    def unit_keep(kind, k):
        mine = pl.ds(pl.multiple_of(core * units, units), units)
        return pltpu.make_async_copy(
            fulls[kind].at[k, :, :, mine], halves[kind].at[0, k], ulocal_sem.at[kind, k]
        )

    def share(g, c):
        for kind in range(2):
            @pl.when(jnp.logical_and(g >= 0, 2 * g >= cols if kind == 1 else 2 * g < cols))
            def _():
                k = lax.rem(2 * g + c, cols)
                unit_send(kind, k).start()
                unit_keep(kind, k).start()

    def gather(kind, k):
        return pltpu.make_async_remote_copy(
            src_ref=sources[kind], dst_ref=panels[kind].at[0, k],
            send_sem=gsend_sem.at[kind, k], recv_sem=grecv_sem.at[kind, k],
            device_id={"col": lax.rem(me + cols - k, cols)}, device_id_type=MESH,
        )

    for kind in range(2):
        for k in range(1, cols):
            gather(kind, k).start()
    own_copies = [
        pltpu.make_async_copy(sources[kind], panels[kind].at[0, 0], local_sem.at[kind])
        for kind in range(2)
    ]
    for copy in own_copies:
        copy.start()
    for copy in own_copies:
        copy.wait()
    for kind in range(2):
        partner(kind, 0).start()

    def weights_copy(kind, part):
        if kind == 0:
            src = win_ref.at[:, pl.ds(part * width, width)]
            return pltpu.make_async_copy(src, win_buf, load_sem.at[0])
        src = wout_ref.at[pl.ds(part * width, width), :]
        return pltpu.make_async_copy(src, wout_buf, load_sem.at[0])

    def tokens_copy(kind, k):
        return pltpu.make_async_copy(panels[kind].at[0, k], tok_buf, load_sem.at[1])

    def load(kind, k, part):
        weights_copy(kind, part).start()
        if part == 0:
            for slot in range(1, cols):
                @pl.when(k == slot)
                def _():
                    gather(kind, slot).wait_recv()
                    partner(kind, slot).start()
            tokens_copy(kind, k).start()

    def multiply(kind, k, part, half, chain):
        weights_copy(kind, part).wait()
        if part == 0:
            tokens_copy(kind, k).wait()
        step = min(width, 256)

        @pl.loop(0, width // step)
        def _(i):
            at = pl.multiple_of(i * step, step)
            if kind == 0:
                out = jnp.dot(tok_buf[...], win_buf[:, pl.ds(at, step)], preferred_element_type=F32)
            else:
                out = lax.dot_general(
                    tok_buf[...], wout_buf[pl.ds(at, step), :], (((1,), (1,)), ((), ())),
                    preferred_element_type=F32,
                )
            to = pl.multiple_of(part * width + i * step, step)
            parts[half, chain, :, :, pl.ds(to, step)] = out.astype(BF16).reshape(n, shard, step)

    def place(d):
        return z if d == 0 else n - 1 - z

    def real(d, q):
        return q if d == 0 else n - 1 - q

    def forms(s, d):
        p = place(d)
        if s == n:
            return p < n - 1, p >= 1
        return jnp.logical_and(p < n - 1, p < s), jnp.logical_and(p >= 1, p - 1 < s)

    def passes_on(s, d):
        p = place(d)
        return jnp.logical_and(p < n - 1, p >= s), jnp.logical_and(p >= 1, p - 1 >= s)

    def both(a, b):
        return jnp.logical_and(a, b)

    def copy_of(src, dst, s, c, d):
        return pltpu.make_async_remote_copy(
            src_ref=src, dst_ref=dst, send_sem=send_sem.at[s - 1, c, d],
            recv_sem=recv_sem.at[s - 1, c, d],
            device_id={"row": z + 1 if d == 0 else z - 1}, device_id_type=MESH,
        )

    def any_copy(s, c, d):
        return copy_of(stage.at[c], stage.at[c], s, c, d)

    def active(g, s, d, sending):
        which = 0 if sending else 1
        fresh = both(forms(s, d)[which], both(g >= 0, g < cols))
        if s > n - 2:
            return fresh
        old = both(passes_on(s, d)[which], both(g >= 1, g <= cols))
        return jnp.logical_or(fresh, old)

    def wait_recv(g, s, c):
        for d in range(2):
            @pl.when(active(g, s, d, False))
            def _():
                any_copy(s, c, d).wait_recv()

    def wait_send(g, s, c):
        for d in range(2):
            @pl.when(active(g, s, d, True))
            def _():
                any_copy(s, c, d).wait_send()

    def arrive(g, s, c):
        if s == 1:
            wait_recv(g - 1, n, c)
        else:
            wait_recv(g, s - 1, c)

    def pass_on(g, s, c):
        for d in range(2):
            for kind in range(2):
                early = 2 * (g - 1) >= cols if kind == 1 else 2 * (g - 1) < cols

                @pl.when(both(both(passes_on(s, d)[0], g >= 1), early))
                def _():
                    k = lax.rem(2 * (g - 1) + c, cols)
                    slot = fulls[kind].at[k, real(d, place(d) - s)]
                    copy_of(slot, slot, s, c, d).start()

    def tick(g, s, c):
        half = lax.rem(g, 2)
        arrive(g, s, c)
        wait_send(g - 1, s, c)
        if s <= n - 2:
            pass_on(g, s, c)
        if s == n - 1:
            share(g - 1, c)
        for d in range(2):
            @pl.when(forms(s, d)[0])
            def _():
                p = place(d)
                j = real(d, n - s + p)

                if s > 1:
                    @pl.when(p >= 1)
                    def _():
                        @pl.loop(0, hidden // strip)
                        def _(i):
                            at = pl.ds(pl.multiple_of(i * strip, strip), strip)
                            own = parts[half, c, j, :, at].astype(F32)
                            got = land[s - 2, c, d, :, at].astype(F32)
                            outgo[s - 1, c, d, :, at] = (own + got).astype(BF16)

                @pl.when(p == 0)
                def _():
                    outgo[s - 1, c, d] = parts[half, c, j]

                copy_of(outgo.at[s - 1, c, d], land.at[s - 1, c, d], s, c, d).start()

    def finish(g, c):
        half = lax.rem(g, 2)
        arrive(g, n, c)
        wait_send(g - 1, n, c)
        k = lax.rem(2 * g + c, cols)

        def total(at):
            own = parts[half, c, z, :, at].astype(F32)
            from_left = jnp.where(z > 0, land[n - 2, c, 0, :, at].astype(F32), 0.0)
            from_right = jnp.where(z < n - 1, land[n - 2, c, 1, :, at].astype(F32), 0.0)
            return own + from_left + from_right

        @pl.when(2 * g < cols)
        def _():
            @pl.loop(0, hidden // strip)
            def _(i):
                at = pl.ds(pl.multiple_of(i * strip, strip), strip)
                activated, steep = gelu_parts(total(at))
                slope[k, :, at] = steep
                stage[c, :, at] = activated.astype(BF16)

        @pl.when(2 * g >= cols)
        def _():
            @pl.loop(0, hidden // strip)
            def _(i):
                at = pl.ds(pl.multiple_of(i * strip, strip), strip)
                stage[c, :, at] = (total(at) * slope[k, :, at]).astype(BF16)

        for kind in range(2):
            @pl.when(2 * g >= cols if kind == 1 else 2 * g < cols)
            def _():
                slot = fulls[kind].at[k, z]
                for d in range(2):
                    @pl.when(forms(n, d)[0])
                    def _():
                        copy_of(stage.at[c], slot, n, c, d).start()
                keep = pltpu.make_async_copy(stage.at[c], slot, local_sem.at[0])
                keep.start()
                keep.wait()

    for c in range(2):
        for part in range(n):
            load(0, c, part)
            multiply(0, c, part, 0, c)
        if c == 0:
            tick(jnp.int32(0), 1, 0)

    @pl.loop(0, cols)
    def _(g):
        for s in range(1, n + 1):
            for c in range(2):
                piece = (s - 1) * 2 + c
                chain, part = piece // n, piece % n
                k = lax.rem(2 * (g + 1) + chain, cols)
                ahead_in = 2 * (g + 1) < cols
                ahead_out = both(2 * (g + 1) >= cols, g < cols - 1)
                for kind, ahead in enumerate((ahead_in, ahead_out)):
                    @pl.when(ahead)
                    def _():
                        load(kind, k, part)
                if s == n:
                    finish(g, c)
                elif s == 1 and c == 0:
                    @pl.when(g > 0)
                    def _():
                        tick(g, s, c)
                else:
                    tick(g, s, c)
                for kind, ahead in enumerate((ahead_in, ahead_out)):
                    @pl.when(ahead)
                    def _():
                        multiply(kind, k, part, lax.rem(g + 1, 2), chain)

    last = jnp.int32(cols)
    for s in range(1, n - 1):
        for c in range(2):
            arrive(last, s, c)
            wait_send(last - 1, s, c)
            pass_on(last, s, c)
    for c in range(2):
        if n > 2:
            wait_recv(last, n - 2, c)
        else:
            wait_recv(last - 1, n, c)
        share(last - 1, c)
        for s in range(1, n - 1):
            wait_send(last, s, c)
        for s in (n - 1, n):
            wait_send(last - 1, s, c)
    for kind in range(2):
        for k in range(1, cols):
            gather(kind, k).wait_send()
        for k in range(cols):
            partner(kind, k).wait()
            unit_send(kind, k).wait()
            unit_keep(kind, k).wait()


def line_call(n, cols, tokens, out_grad, weight_in, weight_out):
    rows, depth = tokens.shape
    hidden = weight_in.shape[1]
    shard, width = rows // n, hidden // n
    return pl.pallas_call(
        functools.partial(line_kernel, n, cols),
        out_shape=[
            jax.ShapeDtypeStruct((2, cols, rows, depth), BF16),
            jax.ShapeDtypeStruct((2, cols, rows, depth), BF16),
            jax.ShapeDtypeStruct((cols, n, shard, hidden), BF16),
            jax.ShapeDtypeStruct((cols, n, shard, hidden), BF16),
            jax.ShapeDtypeStruct((2, cols, n, shard, hidden // 2), BF16),
            jax.ShapeDtypeStruct((2, cols, n, shard, hidden // 2), BF16),
        ],
        in_specs=[pl.BlockSpec(memory_space=pl.ANY)] * 4,
        out_specs=[pl.BlockSpec(memory_space=pl.ANY)] * 6,
        scratch_shapes=[
            pltpu.VMEM((2, 2, n, shard, hidden), BF16),
            pltpu.VMEM((n - 1, 2, 2, shard, hidden), BF16),
            pltpu.VMEM((n - 1, 2, 2, shard, hidden), BF16),
            pltpu.VMEM((2, shard, hidden), BF16),
            pltpu.VMEM((cols, shard, hidden), F32),
            pltpu.VMEM((rows, depth), BF16),
            pltpu.VMEM((depth, width), BF16),
            pltpu.VMEM((width, depth), BF16),
            pltpu.SemaphoreType.DMA((n, 2, 2)),
            pltpu.SemaphoreType.DMA((n, 2, 2)),
            pltpu.SemaphoreType.DMA((2, cols)),
            pltpu.SemaphoreType.DMA((2, cols)),
            pltpu.SemaphoreType.DMA((2,)),
            pltpu.SemaphoreType.DMA((2,)),
            pltpu.SemaphoreType.DMA((2, cols)),
            pltpu.SemaphoreType.DMA((2, cols)),
            pltpu.SemaphoreType.DMA((2, cols)),
            pltpu.SemaphoreType.DMA((2, cols)),
            pltpu.SemaphoreType.DMA((2, cols)),
        ],
        compiler_params=pltpu.CompilerParams(
            collective_id=0, has_side_effects=True, vmem_limit_bytes=56 * 2**20
        ),
    )(tokens, out_grad, weight_in, weight_out)


def shards(tokens, out_grad, weight_in, weight_out):
    cols, n = lax.axis_size("col"), lax.axis_size("row")
    factor = 1.0 / math.sqrt(tokens.shape[0] * cols * lax.axis_size("dp"))
    hidden = weight_in.shape[1]
    tok, cot, act, dpre, act_units, dpre_units = line_call(
        n, cols, tokens, out_grad, weight_in, weight_out
    )
    tok, cot = tok.reshape(-1, tok.shape[-1]), cot.reshape(-1, cot.shape[-1])
    act, dpre = act.reshape(-1, hidden), dpre.reshape(-1, hidden)
    act_units = act_units.reshape(-1, hidden // 2)
    dpre_units = dpre_units.reshape(-1, hidden // 2)

    def sent(part):
        part = part.astype(BF16).reshape(cols, -1, part.shape[-1])
        rings = [[(i, (i + k) % cols) for i in range(cols)] for k in range(1, cols)]
        return [part[0]] + [lax.ppermute(part[k + 1], "col", rings[k]) for k in range(cols - 1)]

    def summed(parts):
        total = parts[0].astype(F32)
        for part in parts[1:]:
            total = total + part.astype(F32)
        return total.astype(BF16)

    def across(left, right):
        return lax.dot_general(left, right, (((0,), (0,)), ((), ())), preferred_element_type=F32)

    mixed = sent(jnp.dot(act, weight_out, preferred_element_type=F32))
    token_grad = sent(
        lax.dot_general(dpre, weight_in, (((1,), (1,)), ((), ())), preferred_element_type=F32)
    )
    mixed[0], token_grad[0], act_units, tok = lax.optimization_barrier(
        (mixed[0], token_grad[0], act_units, tok)
    )
    grad_out = across(act_units, cot) * factor
    grad_in = across(tok, dpre_units) * factor
    mixed, token_grad, grad_out, grad_in = lax.optimization_barrier(
        (mixed, token_grad, grad_out, grad_in)
    )
    return (summed(mixed), summed(token_grad), grad_in, grad_out)


def solution(mesh):
    placed = (P(("col", "dp"), "row"), P(("col", "dp"), "row"), P("row", "col"), P("col", "row"))
    return jax.shard_map(
        shards,
        mesh=mesh,
        in_specs=placed,
        out_specs=(
            P(("col", "dp"), "row"),
            P(("col", "dp"), "row"),
            P("row", ("col", "dp")),
            P(("col", "dp"), "row"),
        ),
        check_vma=False,
    )
```

```python
import functools
import math

import jax
import jax.numpy as jnp
from jax import lax
from jax.experimental import pallas as pl
from jax.experimental.pallas import tpu as pltpu
from jax.sharding import PartitionSpec as P

F32, BF16 = jnp.float32, jnp.bfloat16
MESH = pl.DeviceIdType.MESH


def gelu_parts(pre):
    cdf = 0.5 * (1.0 + jax.scipy.special.erf(pre * (1.0 / math.sqrt(2.0))))
    activated = pre * cdf
    slope = cdf + pre * jnp.exp(-0.5 * pre * pre) * (1.0 / math.sqrt(2.0 * math.pi))
    return (activated, slope)


def line_kernel(
    n, cols, tok_ref, cot_ref, win_ref, wout_ref, ptok_ref, pcot_ref,
    act_ref, dpre_ref, uact_ref, udpre_ref, parts, outgo, land, stage, slope, tok_buf, win_buf, wout_buf,
    send_sem, recv_sem, gsend_sem, grecv_sem, local_sem, load_sem,
    psend_sem, precv_sem, usend_sem, urecv_sem, ulocal_sem,
):
    rows, hidden = tok_ref.shape[0], win_ref.shape[1]
    shard, width = rows // n, hidden // n
    z, me = lax.axis_index("row"), lax.axis_index("col")
    strip = min(1024, hidden)
    core, units = lax.axis_index("dp"), hidden // 2

    barrier = pltpu.get_barrier_semaphore()

    @pl.when(z > 0)
    def _():
        pl.semaphore_signal(barrier, inc=1, device_id={"row": z - 1}, device_id_type=MESH)

    @pl.when(z < n - 1)
    def _():
        pl.semaphore_signal(barrier, inc=1, device_id={"row": z + 1}, device_id_type=MESH)

    pl.semaphore_signal(barrier, inc=1, device_id={"dp": 1 - core}, device_id_type=MESH)
    for k in range(1, cols):
        peer = lax.rem(me + k, cols)
        pl.semaphore_signal(barrier, inc=1, device_id={"col": peer}, device_id_type=MESH)

    @pl.when(jnp.logical_or(z == 0, z == n - 1))
    def _():
        pl.semaphore_wait(barrier, cols + 1)

    @pl.when(jnp.logical_and(z > 0, z < n - 1))
    def _():
        pl.semaphore_wait(barrier, cols + 2)

    sources, panels = (tok_ref, cot_ref), (ptok_ref, pcot_ref)

    fulls, halves = (act_ref, dpre_ref), (uact_ref, udpre_ref)

    def partner(kind, k):
        return pltpu.make_async_remote_copy(
            src_ref=panels[kind].at[0, k], dst_ref=panels[kind].at[1, k],
            send_sem=psend_sem.at[kind, k], recv_sem=precv_sem.at[kind, k],
            device_id={"dp": 1 - core}, device_id_type=MESH,
        )

    def unit_send(kind, k):
        theirs = pl.ds(pl.multiple_of((1 - core) * units, units), units)
        return pltpu.make_async_remote_copy(
            src_ref=fulls[kind].at[k, :, :, theirs], dst_ref=halves[kind].at[1, k],
            send_sem=usend_sem.at[kind, k], recv_sem=urecv_sem.at[kind, k],
            device_id={"dp": 1 - core}, device_id_type=MESH,
        )

    def unit_keep(kind, k):
        mine = pl.ds(pl.multiple_of(core * units, units), units)
        return pltpu.make_async_copy(
            fulls[kind].at[k, :, :, mine], halves[kind].at[0, k], ulocal_sem.at[kind, k]
        )

    def share(g, c):
        for kind in range(2):
            @pl.when(jnp.logical_and(g >= 0, 2 * g >= cols if kind == 1 else 2 * g < cols))
            def _():
                k = lax.rem(2 * g + c, cols)
                unit_send(kind, k).start()
                unit_keep(kind, k).start()

    def gather(kind, k):
        return pltpu.make_async_remote_copy(
            src_ref=sources[kind], dst_ref=panels[kind].at[0, k],
            send_sem=gsend_sem.at[kind, k], recv_sem=grecv_sem.at[kind, k],
            device_id={"col": lax.rem(me + cols - k, cols)}, device_id_type=MESH,
        )

    for kind in range(2):
        for k in range(1, cols):
            gather(kind, k).start()
    own_copies = [
        pltpu.make_async_copy(sources[kind], panels[kind].at[0, 0], local_sem.at[kind])
        for kind in range(2)
    ]
    for copy in own_copies:
        copy.start()
    for copy in own_copies:
        copy.wait()
    for kind in range(2):
        partner(kind, 0).start()

    def weights_copy(kind, part):
        if kind == 0:
            src = win_ref.at[:, pl.ds(part * width, width)]
            return pltpu.make_async_copy(src, win_buf, load_sem.at[0])
        src = wout_ref.at[pl.ds(part * width, width), :]
        return pltpu.make_async_copy(src, wout_buf, load_sem.at[0])

    def tokens_copy(kind, k):
        return pltpu.make_async_copy(panels[kind].at[0, k], tok_buf, load_sem.at[1])

    def load(kind, k, part):
        weights_copy(kind, part).start()
        if part == 0:
            for slot in range(1, cols):
                @pl.when(k == slot)
                def _():
                    gather(kind, slot).wait_recv()
                    partner(kind, slot).start()
            tokens_copy(kind, k).start()

    def multiply(kind, k, part, half, chain):
        weights_copy(kind, part).wait()
        if part == 0:
            tokens_copy(kind, k).wait()
        step = min(width, 512)

        @pl.loop(0, width // step)
        def _(i):
            at = pl.multiple_of(i * step, step)
            if kind == 0:
                out = jnp.dot(tok_buf[...], win_buf[:, pl.ds(at, step)], preferred_element_type=F32)
            else:
                out = lax.dot_general(
                    tok_buf[...], wout_buf[pl.ds(at, step), :], (((1,), (1,)), ((), ())),
                    preferred_element_type=F32,
                )
            to = pl.multiple_of(part * width + i * step, step)
            parts[half, chain, :, :, pl.ds(to, step)] = out.astype(BF16).reshape(n, shard, step)

    def place(d):
        return z if d == 0 else n - 1 - z

    def real(d, q):
        return q if d == 0 else n - 1 - q

    def forms(s, d):
        p = place(d)
        if s == n:
            return p < n - 1, p >= 1
        return jnp.logical_and(p < n - 1, p < s), jnp.logical_and(p >= 1, p - 1 < s)

    def passes_on(s, d):
        p = place(d)
        return jnp.logical_and(p < n - 1, p >= s), jnp.logical_and(p >= 1, p - 1 >= s)

    def both(a, b):
        return jnp.logical_and(a, b)

    def copy_of(src, dst, s, c, d):
        return pltpu.make_async_remote_copy(
            src_ref=src, dst_ref=dst, send_sem=send_sem.at[s - 1, c, d],
            recv_sem=recv_sem.at[s - 1, c, d],
            device_id={"row": z + 1 if d == 0 else z - 1}, device_id_type=MESH,
        )

    def any_copy(s, c, d):
        return copy_of(stage.at[c], stage.at[c], s, c, d)

    def active(g, s, d, sending):
        which = 0 if sending else 1
        fresh = both(forms(s, d)[which], both(g >= 0, g < cols))
        if s > n - 2:
            return fresh
        old = both(passes_on(s, d)[which], both(g >= 1, g <= cols))
        return jnp.logical_or(fresh, old)

    def wait_recv(g, s, c):
        for d in range(2):
            @pl.when(active(g, s, d, False))
            def _():
                any_copy(s, c, d).wait_recv()

    def wait_send(g, s, c):
        for d in range(2):
            @pl.when(active(g, s, d, True))
            def _():
                any_copy(s, c, d).wait_send()

    def arrive(g, s, c):
        if s == 1:
            wait_recv(g - 1, n, c)
        else:
            wait_recv(g, s - 1, c)

    def pass_on(g, s, c):
        for d in range(2):
            for kind in range(2):
                early = 2 * (g - 1) >= cols if kind == 1 else 2 * (g - 1) < cols

                @pl.when(both(both(passes_on(s, d)[0], g >= 1), early))
                def _():
                    k = lax.rem(2 * (g - 1) + c, cols)
                    slot = fulls[kind].at[k, real(d, place(d) - s)]
                    copy_of(slot, slot, s, c, d).start()

    def tick(g, s, c):
        half = lax.rem(g, 2)
        arrive(g, s, c)
        wait_send(g - 1, s, c)
        if s <= n - 2:
            pass_on(g, s, c)
        if s == n - 1:
            share(g - 1, c)
        for d in range(2):
            @pl.when(forms(s, d)[0])
            def _():
                p = place(d)
                j = real(d, n - s + p)

                if s > 1:
                    @pl.when(p >= 1)
                    def _():
                        @pl.loop(0, hidden // strip)
                        def _(i):
                            at = pl.ds(pl.multiple_of(i * strip, strip), strip)
                            own = parts[half, c, j, :, at].astype(F32)
                            got = land[s - 2, c, d, :, at].astype(F32)
                            outgo[s - 1, c, d, :, at] = (own + got).astype(BF16)

                @pl.when(p == 0)
                def _():
                    outgo[s - 1, c, d] = parts[half, c, j]

                copy_of(outgo.at[s - 1, c, d], land.at[s - 1, c, d], s, c, d).start()

    def finish(g, c):
        half = lax.rem(g, 2)
        arrive(g, n, c)
        wait_send(g - 1, n, c)
        k = lax.rem(2 * g + c, cols)

        def total(at):
            own = parts[half, c, z, :, at].astype(F32)
            from_left = jnp.where(z > 0, land[n - 2, c, 0, :, at].astype(F32), 0.0)
            from_right = jnp.where(z < n - 1, land[n - 2, c, 1, :, at].astype(F32), 0.0)
            return own + from_left + from_right

        @pl.when(2 * g < cols)
        def _():
            @pl.loop(0, hidden // strip)
            def _(i):
                at = pl.ds(pl.multiple_of(i * strip, strip), strip)
                activated, steep = gelu_parts(total(at))
                slope[k, :, at] = steep
                stage[c, :, at] = activated.astype(BF16)

        @pl.when(2 * g >= cols)
        def _():
            @pl.loop(0, hidden // strip)
            def _(i):
                at = pl.ds(pl.multiple_of(i * strip, strip), strip)
                stage[c, :, at] = (total(at) * slope[k, :, at]).astype(BF16)

        for kind in range(2):
            @pl.when(2 * g >= cols if kind == 1 else 2 * g < cols)
            def _():
                slot = fulls[kind].at[k, z]
                for d in range(2):
                    @pl.when(forms(n, d)[0])
                    def _():
                        copy_of(stage.at[c], slot, n, c, d).start()
                keep = pltpu.make_async_copy(stage.at[c], slot, local_sem.at[0])
                keep.start()
                keep.wait()

    for c in range(2):
        for part in range(n):
            load(0, c, part)
            multiply(0, c, part, 0, c)
        if c == 0:
            tick(jnp.int32(0), 1, 0)

    @pl.loop(0, cols)
    def _(g):
        for s in range(1, n + 1):
            for c in range(2):
                piece = (s - 1) * 2 + c
                chain, part = piece // n, piece % n
                k = lax.rem(2 * (g + 1) + chain, cols)
                ahead_in = 2 * (g + 1) < cols
                ahead_out = both(2 * (g + 1) >= cols, g < cols - 1)
                for kind, ahead in enumerate((ahead_in, ahead_out)):
                    @pl.when(ahead)
                    def _():
                        load(kind, k, part)
                if s == n:
                    finish(g, c)
                elif s == 1 and c == 0:
                    @pl.when(g > 0)
                    def _():
                        tick(g, s, c)
                else:
                    tick(g, s, c)
                for kind, ahead in enumerate((ahead_in, ahead_out)):
                    @pl.when(ahead)
                    def _():
                        multiply(kind, k, part, lax.rem(g + 1, 2), chain)

    last = jnp.int32(cols)
    for s in range(1, n - 1):
        for c in range(2):
            arrive(last, s, c)
            wait_send(last - 1, s, c)
            pass_on(last, s, c)
    for c in range(2):
        if n > 2:
            wait_recv(last, n - 2, c)
        else:
            wait_recv(last - 1, n, c)
        share(last - 1, c)
        for s in range(1, n - 1):
            wait_send(last, s, c)
        for s in (n - 1, n):
            wait_send(last - 1, s, c)
    for kind in range(2):
        for k in range(1, cols):
            gather(kind, k).wait_send()
        for k in range(cols):
            partner(kind, k).wait()
            unit_send(kind, k).wait()
            unit_keep(kind, k).wait()


def line_call(n, cols, tokens, out_grad, weight_in, weight_out):
    rows, depth = tokens.shape
    hidden = weight_in.shape[1]
    shard, width = rows // n, hidden // n
    return pl.pallas_call(
        functools.partial(line_kernel, n, cols),
        out_shape=[
            jax.ShapeDtypeStruct((2, cols, rows, depth), BF16),
            jax.ShapeDtypeStruct((2, cols, rows, depth), BF16),
            jax.ShapeDtypeStruct((cols, n, shard, hidden), BF16),
            jax.ShapeDtypeStruct((cols, n, shard, hidden), BF16),
            jax.ShapeDtypeStruct((2, cols, n, shard, hidden // 2), BF16),
            jax.ShapeDtypeStruct((2, cols, n, shard, hidden // 2), BF16),
        ],
        in_specs=[pl.BlockSpec(memory_space=pl.ANY)] * 4,
        out_specs=[pl.BlockSpec(memory_space=pl.ANY)] * 6,
        scratch_shapes=[
            pltpu.VMEM((2, 2, n, shard, hidden), BF16),
            pltpu.VMEM((n - 1, 2, 2, shard, hidden), BF16),
            pltpu.VMEM((n - 1, 2, 2, shard, hidden), BF16),
            pltpu.VMEM((2, shard, hidden), BF16),
            pltpu.VMEM((cols, shard, hidden), F32),
            pltpu.VMEM((rows, depth), BF16),
            pltpu.VMEM((depth, width), BF16),
            pltpu.VMEM((width, depth), BF16),
            pltpu.SemaphoreType.DMA((n, 2, 2)),
            pltpu.SemaphoreType.DMA((n, 2, 2)),
            pltpu.SemaphoreType.DMA((2, cols)),
            pltpu.SemaphoreType.DMA((2, cols)),
            pltpu.SemaphoreType.DMA((2,)),
            pltpu.SemaphoreType.DMA((2,)),
            pltpu.SemaphoreType.DMA((2, cols)),
            pltpu.SemaphoreType.DMA((2, cols)),
            pltpu.SemaphoreType.DMA((2, cols)),
            pltpu.SemaphoreType.DMA((2, cols)),
            pltpu.SemaphoreType.DMA((2, cols)),
        ],
        compiler_params=pltpu.CompilerParams(
            collective_id=0, has_side_effects=True, vmem_limit_bytes=56 * 2**20
        ),
    )(tokens, out_grad, weight_in, weight_out)


def shards(tokens, out_grad, weight_in, weight_out):
    cols, n = lax.axis_size("col"), lax.axis_size("row")
    factor = 1.0 / math.sqrt(tokens.shape[0] * cols * lax.axis_size("dp"))
    hidden = weight_in.shape[1]
    tok, cot, act, dpre, act_units, dpre_units = line_call(
        n, cols, tokens, out_grad, weight_in, weight_out
    )
    tok, cot = tok.reshape(-1, tok.shape[-1]), cot.reshape(-1, cot.shape[-1])
    act, dpre = act.reshape(-1, hidden), dpre.reshape(-1, hidden)
    act_units = act_units.reshape(-1, hidden // 2)
    dpre_units = dpre_units.reshape(-1, hidden // 2)

    def sent(part):
        part = part.astype(BF16).reshape(cols, -1, part.shape[-1])
        rings = [[(i, (i + k) % cols) for i in range(cols)] for k in range(1, cols)]
        return [part[0]] + [lax.ppermute(part[k + 1], "col", rings[k]) for k in range(cols - 1)]

    def summed(parts):
        total = parts[0].astype(F32)
        for part in parts[1:]:
            total = total + part.astype(F32)
        return total.astype(BF16)

    def across(left, right):
        return lax.dot_general(left, right, (((0,), (0,)), ((), ())), preferred_element_type=F32)

    mixed = sent(jnp.dot(act, weight_out, preferred_element_type=F32))
    token_grad = sent(
        lax.dot_general(dpre, weight_in, (((1,), (1,)), ((), ())), preferred_element_type=F32)
    )
    mixed[0], token_grad[0], act_units, tok = lax.optimization_barrier(
        (mixed[0], token_grad[0], act_units, tok)
    )
    grad_out = across(act_units, cot) * factor
    grad_in = across(tok, dpre_units) * factor
    mixed, token_grad, grad_out, grad_in = lax.optimization_barrier(
        (mixed, token_grad, grad_out, grad_in)
    )
    return (summed(mixed), summed(token_grad), grad_in, grad_out)


def solution(mesh):
    placed = (P(("col", "dp"), "row"), P(("col", "dp"), "row"), P("row", "col"), P("col", "row"))
    return jax.shard_map(
        shards,
        mesh=mesh,
        in_specs=placed,
        out_specs=(
            P(("col", "dp"), "row"),
            P(("col", "dp"), "row"),
            P("row", ("col", "dp")),
            P(("col", "dp"), "row"),
        ),
        check_vma=False,
    )
```
